256 devices in a mesh: dp: 8 (over x, core), tensor: 32 (over z, y).
Axes of the slice: x: 4, y: 4, z: 8, core: 2. Of those that a mesh axis runs over, the one named last changes fastest.
Arguments:
- inputs: bfloat16 [4, 128, 8192], P(None, 'tensor', 'dp'), may hold values from -6 to 6
- grad_out: bfloat16 [4, 128, 8192], P(None, 'tensor', 'dp'), may hold values from -6 to 6
- gate_pre: bfloat16 [4, 128, 28672], P(None, 'dp', 'tensor'), may hold values from -6 to 6
- up_pre: bfloat16 [4, 128, 28672], P(None, 'dp', 'tensor'), may hold values from -6 to 6
- gate_weight: bfloat16 [8192, 28672], P('dp', 'tensor'), may hold values from -0.0625 to 0.0625
- up_weight: bfloat16 [8192, 28672], P('dp', 'tensor'), may hold values from -0.0625 to 0.0625
- down_weight: bfloat16 [8192, 28672], P('dp', 'tensor'), may hold values from -0.03125 to 0.03125
Outputs:
- input_grads: bfloat16 [4, 128, 8192], P(None, 'tensor', 'dp')
- gate_grad: bfloat16 [8192, 28672], P('dp', 'tensor')
- up_grad: bfloat16 [8192, 28672], P('dp', 'tensor')
- down_grad: bfloat16 [8192, 28672], P('dp', 'tensor')
The draws below stay inside these ranges and needn't reach their ends.
All inputs are finite; a program needn't handle non-finite values.
Results may differ from the reference program's by a relative error of at most 0.0049.
Values may be sent and summed in bfloat16 or wider, within the bound.
No kernel may reach another device: no remote copies, remote signals or barrier semaphores. Data moves between devices by JAX's collectives and lax.ppermute only.
A program may use at most 128 MiB of HBM per device.

```python
import jax
import jax.numpy as jnp
from jax import lax

D = 8192
FF = 28672
G = 4
TOKENS = 128


def block_scale(own_key, dims, shards, smallest, largest):
    gain = 1.0
    for position, parts in shards:
        draws = jax.random.uniform(jax.random.fold_in(jax.random.fold_in(own_key, 6), position), (parts,), jnp.float32, smallest / len(shards), largest / len(shards))
        gain = gain * jnp.repeat(jnp.exp(draws), dims[position] // parts).reshape((-1,) + (1,) * (len(dims) - 1 - position))
    return gain


def noise(key, shape, width, bound, split=(), dtype=jnp.bfloat16):
    level = block_scale(key, shape, split, -0.22, 0.18) if split else 1.0
    array = jax.random.normal(key, shape, jnp.float32) * width * level
    return jnp.minimum(jnp.maximum(array, -bound), bound).astype(dtype)


def setup_inputs(seed: int = 0) -> dict:
    splits = jax.random.split(jax.random.key(seed), 8)
    return {
        "inputs": noise(splits[0], (G, TOKENS, D), 1.0, 6.0, ((1, 32), (2, 8))),
        "grad_out": noise(splits[1], (G, TOKENS, D), 1.0, 6.0, ((1, 32), (2, 8))),
        "gate_pre": noise(splits[2], (G, TOKENS, FF), 1.0, 6.0, ((1, 8), (2, 32))),
        "up_pre": noise(splits[3], (G, TOKENS, FF), 1.0, 6.0, ((1, 8), (2, 32))),
        "gate_weight": noise(splits[4], (D, FF), D ** -0.5, 0.0625, ((0, 8), (1, 32))),
        "up_weight": noise(splits[5], (D, FF), D ** -0.5, 0.0625, ((0, 8), (1, 32))),
        "down_weight": noise(splits[6], (D, FF), FF ** -0.5, 0.03125, ((0, 8), (1, 32))),
    }


def swish_terms(d_hidden, gate_part, up_part):
    gate_float = gate_part.astype(jnp.float32)
    up_float = up_part.astype(jnp.float32)
    sigmoid_val = jax.nn.sigmoid(gate_float)
    active = gate_float * sigmoid_val
    d_gate = (d_hidden * up_float * sigmoid_val * (1.0 + gate_float * (1.0 - sigmoid_val))).astype(jnp.bfloat16)
    d_up = (d_hidden * active).astype(jnp.bfloat16)
    hidden = (active * up_float).astype(jnp.bfloat16)
    return d_gate, d_up, hidden


def contract_rows(left_arr, right_arr):
    return lax.dot_general(left_arr, right_arr, (((0,), (0,)), ((), ())), preferred_element_type=jnp.float32)


def contract_cols(left_arr, right_arr):
    return lax.dot_general(left_arr, right_arr, (((1,), (1,)), ((), ())), preferred_element_type=jnp.float32)


def reference(inputs, grad_out, gate_pre, up_pre, gate_weight, up_weight, down_weight):
    prefixes = [FF // 2 ** (G - 1 - granule) for granule in range(G)]
    in_grads = []
    d_gates = []
    d_ups = []
    hiddens = []
    for granule in range(G):
        prefix_cols = prefixes[granule]
        d_hidden = jnp.dot(grad_out[granule], down_weight[:, :prefix_cols], preferred_element_type=jnp.float32)
        d_gate, d_up, hidden = swish_terms(d_hidden, gate_pre[granule][:, :prefix_cols], up_pre[granule][:, :prefix_cols])
        input_term = contract_cols(d_gate, gate_weight[:, :prefix_cols]) + contract_cols(d_up, up_weight[:, :prefix_cols])
        in_grads.append(input_term.astype(jnp.bfloat16))
        d_gates.append(d_gate)
        d_ups.append(d_up)
        hiddens.append(hidden)
    gate_blocks = []
    up_blocks = []
    down_blocks = []
    start_col = 0
    for granule in range(G):
        stop_col = prefixes[granule]
        gate_total = jnp.zeros((D, stop_col - start_col), jnp.float32)
        up_total = jnp.zeros((D, stop_col - start_col), jnp.float32)
        down_total = jnp.zeros((D, stop_col - start_col), jnp.float32)
        for later_granule in range(granule, G):
            gate_total = gate_total + contract_rows(inputs[later_granule], d_gates[later_granule][:, start_col:stop_col])
            up_total = up_total + contract_rows(inputs[later_granule], d_ups[later_granule][:, start_col:stop_col])
            down_total = down_total + contract_rows(grad_out[later_granule], hiddens[later_granule][:, start_col:stop_col])
        gate_blocks.append(gate_total.astype(jnp.bfloat16))
        up_blocks.append(up_total.astype(jnp.bfloat16))
        down_blocks.append(down_total.astype(jnp.bfloat16))
        start_col = stop_col
    gate_grad = jnp.concatenate(gate_blocks, axis=1)
    up_grad = jnp.concatenate(up_blocks, axis=1)
    down_grad = jnp.concatenate(down_blocks, axis=1)
    return jnp.stack(in_grads), gate_grad, up_grad, down_grad
```

```python
import functools

import jax
import jax.numpy as jnp
from jax import lax
from jax.experimental import pallas as pl
from jax.experimental.pallas import tpu as pltpu
from jax.sharding import PartitionSpec as P

FF = 28672
G = 4
X, C, Y, Z = 4, 2, 4, 8
BF = jnp.bfloat16
F32 = jnp.float32
VMEM_BYTES = 32 * 1024 * 1024
Z_GROUPS = [
    [(x * C + c) * Y * Z + ((x + dx) % X * C + (c ^ dc)) * Y + y for dc in range(C) for dx in range(X)]
    for x in range(X)
    for c in range(C)
    for y in range(Y)
]
CORE_SWAP = [(d, d ^ 1) for d in range(X * C)]


def from_x(block, step):
    return lax.ppermute(block, "dp", [((d // C + step) % X * C + d % C, d) for d in range(X * C)])


def from_y(block, step):
    return lax.ppermute(block, "tensor", [(t // Y * Y + (t % Y + step) % Y, t) for t in range(Y * Z)])


def swap_core(block):
    return lax.ppermute(block, "dp", CORE_SWAP)


def exchange_z(blocks):
    return lax.all_to_all(blocks, ("dp", "tensor"), 0, 0, axis_index_groups=Z_GROUPS)


def rows_dot(left, right):
    return lax.dot_general(left, right, (((0,), (0,)), ((), ())), preferred_element_type=F32)


def cols_dot(left, right):
    return lax.dot_general(left, right, (((1,), (1,)), ((), ())), preferred_element_type=F32)


def own_tokens(part, y):
    cols = part.shape[-1]
    part = part.reshape(G, Y, 4, cols).transpose(1, 0, 2, 3).reshape(Y, 16, cols)
    return lax.dynamic_slice_in_dim(jnp.concatenate([part, part]), y, Y, 0)


def half_kernel(core, *refs):
    pieces, weight_ref = refs[:Y], refs[Y]
    rows = [p[core * X : core * X + X].reshape(X * 16, p.shape[-1]) for p in pieces]
    part = jnp.dot(jnp.concatenate(rows), weight_ref[...], preferred_element_type=F32)
    if core == 1:
        refs[Y + 1][...] = part
        return
    theirs_ref, own_ref, sent_refs = refs[Y + 1], refs[Y + 2], refs[Y + 3 :]
    part = (part + theirs_ref[...]).reshape(Y, X, 16, part.shape[-1])
    own_ref[...] = part[:, 0]
    for j in range(1, X):
        sent_refs[j - 1][...] = part[:, j].astype(BF)


def half_dot(core, pieces, weight, theirs=()):
    width, cols = weight.shape
    shape = jax.ShapeDtypeStruct((256, cols), F32)
    if core == 0:
        block = (Y, 16, cols)
        shape = [jax.ShapeDtypeStruct(block, F32)] + [jax.ShapeDtypeStruct(block, BF)] * (X - 1)
    vmem = pl.BlockSpec(memory_space=pltpu.VMEM)
    return pl.pallas_call(
        functools.partial(half_kernel, core),
        out_shape=shape,
        in_specs=[vmem] * (Y + 1 + len(theirs)),
        out_specs=jax.tree.map(lambda _: vmem, shape),
        compiler_params=pltpu.CompilerParams(vmem_limit_bytes=VMEM_BYTES),
        cost_estimate=pl.CostEstimate(
            flops=2 * 256 * width * cols, bytes_accessed=2 * width * cols, transcendentals=0
        ),
        name=f"half_{core}",
    )(*pieces, weight, *theirs)


def input_kernel(*refs):
    pieces, (gate_ref, up_ref), (rows_ref, own_ref), sent_refs = (
        refs[:Z],
        refs[Z : Z + 2],
        refs[Z + 2 : Z + 4],
        refs[Z + 4 :],
    )
    for k in range(Z):
        for array in range(2):
            for j in range(Y):
                rows_ref[array, pl.ds((j * Z + k) * 16, 16), :] = pieces[k][array, j]
    for start in range(0, own_ref.shape[1], 256):
        lanes = pl.ds(start, 256)
        term = cols_dot(rows_ref[0], gate_ref[lanes, :]) + cols_dot(rows_ref[1], up_ref[lanes, :])
        own_ref[:, lanes] = term[:128]
        for j in range(1, Y):
            sent_refs[j - 1][:, lanes] = term[128 * j : 128 * j + 128].astype(BF)


def input_terms(pieces, gate_weight, up_weight):
    width, cols = gate_weight.shape
    vmem = pl.BlockSpec(memory_space=pltpu.VMEM)
    return pl.pallas_call(
        input_kernel,
        out_shape=[
            jax.ShapeDtypeStruct((2, 512, cols), BF),
            jax.ShapeDtypeStruct((128, width), F32),
        ]
        + [jax.ShapeDtypeStruct((128, width), BF)] * (Y - 1),
        in_specs=[vmem] * (Z + 2),
        out_specs=[vmem] * (Y + 1),
        compiler_params=pltpu.CompilerParams(vmem_limit_bytes=VMEM_BYTES),
        cost_estimate=pl.CostEstimate(
            flops=4 * 512 * width * cols, bytes_accessed=4 * width * cols, transcendentals=0
        ),
        name="input_terms",
    )(*pieces, gate_weight, up_weight)


def shards(inputs, grad_out, gate_pre, up_pre, gate_weight, up_weight, down_weight):
    width, cols = gate_weight.shape
    tensor = lax.axis_index("tensor")
    prefixes = jnp.array([FF // 2 ** (G - 1 - g) for g in range(G)], jnp.int32)
    live = jnp.repeat(tensor * cols < prefixes, 4)[None, :, None]

    both = jnp.stack([grad_out, inputs]).reshape(2, 16, width)
    both = exchange_z(jnp.broadcast_to(both, (Z, 2, 16, width)))
    gate = own_tokens(gate_pre, tensor % Y).astype(F32)
    up = own_tokens(up_pre, tensor % Y).astype(F32)
    sig = jax.nn.sigmoid(gate)
    gate_factor = jnp.where(live, up * sig * (1.0 + gate * (1.0 - sig)), 0.0)
    up_factor = jnp.where(live, gate * sig, 0.0)
    hidden = (up_factor * up).astype(BF)
    hidden = [hidden] + [from_x(hidden, j) for j in range(1, X)]
    both, hidden = lax.optimization_barrier((both, hidden))
    grad_z, in_z = both[:, 0], both[:, 1]
    grad_y = [grad_z] + [from_y(grad_z, j) for j in range(1, Y)]

    theirs = swap_core(half_dot(1, grad_y, down_weight))
    dhid, *blocks = half_dot(0, grad_y, down_weight, (theirs,))
    for j in range(1, X):
        dhid = dhid + from_x(blocks[j - 1], -j).astype(F32)

    d_own = jnp.stack([dhid * gate_factor, dhid * up_factor]).astype(BF)
    d_x = [d_own] + [from_x(d_own, j) for j in range(1, X)]
    d_other = [swap_core(d) for d in d_x]
    d_other[0], in_z = lax.optimization_barrier((d_other[0], in_z))
    in_y = [in_z] + [from_y(in_z, j) for j in range(1, Y)]
    hidden = jnp.stack(hidden)
    hidden = [hidden, swap_core(hidden)]

    rows, own, *sent = input_terms(d_x + d_other, gate_weight, up_weight)
    sent, grad_y, hidden = lax.optimization_barrier((sent, grad_y, hidden))
    got = [from_y(sent[j - 1], -j) for j in range(1, Y)]
    in_rows = jnp.stack(in_y).reshape(512, width)
    grad_rows = jnp.stack(grad_y).reshape(512, width)
    hidden = jnp.stack(hidden).reshape(Z, Y, 16, cols).transpose(1, 0, 2, 3).reshape(512, cols)
    total = own
    for g in got:
        total = total + g.astype(F32)
    total, rows, in_rows, grad_rows, hidden = lax.optimization_barrier(
        (total.astype(BF), rows, in_rows, grad_rows, hidden)
    )
    total = exchange_z(total.reshape(Z, 16, width))
    gate_grad = rows_dot(in_rows, rows[0]).astype(BF)
    up_grad = rows_dot(in_rows, rows[1]).astype(BF)
    down_grad = rows_dot(grad_rows, hidden).astype(BF)
    in_grads = total.astype(F32).sum(0).astype(BF).reshape(G, 4, width)
    return in_grads, gate_grad, up_grad, down_grad


def solution(mesh):
    tokens = P(None, "tensor", "dp")
    hidden = P(None, "dp", "tensor")
    weight = P("dp", "tensor")
    return jax.shard_map(
        shards,
        mesh=mesh,
        in_specs=(tokens, tokens, hidden, hidden, weight, weight, weight),
        out_specs=(tokens, weight, weight, weight),
        check_vma=False,
    )
```

```python
import functools

import jax
import jax.numpy as jnp
from jax import lax
from jax.experimental import pallas as pl
from jax.experimental.pallas import tpu as pltpu
from jax.sharding import PartitionSpec as P

FF = 28672
G = 4
X, C, Y, Z = 4, 2, 4, 8
BF = jnp.bfloat16
F32 = jnp.float32
MIB = 1024 * 1024
BAND = 256
Z_GROUPS = [
    [(x * C + c) * Y * Z + ((x + dx) % X * C + (c ^ dc)) * Y + y for dc in range(C) for dx in range(X)]
    for x in range(X)
    for c in range(C)
    for y in range(Y)
]
CORE_SWAP = [(d, d ^ 1) for d in range(X * C)]


def from_x(block, step):
    return lax.ppermute(block, "dp", [((d // C + step) % X * C + d % C, d) for d in range(X * C)])


def from_y(block, step):
    return lax.ppermute(block, "tensor", [(t // Y * Y + (t % Y + step) % Y, t) for t in range(Y * Z)])


def swap_core(block):
    return lax.ppermute(block, "dp", CORE_SWAP)


def exchange_z(blocks):
    return lax.all_to_all(blocks, ("dp", "tensor"), 0, 0, axis_index_groups=Z_GROUPS)


def rows_dot(left, right):
    return lax.dot_general(left, right, (((0,), (0,)), ((), ())), preferred_element_type=F32)


def cols_dot(left, right):
    return lax.dot_general(left, right, (((1,), (1,)), ((), ())), preferred_element_type=F32)


def own_tokens(part, y):
    cols = part.shape[-1]
    part = part.reshape(G, Y, 4, cols).transpose(1, 0, 2, 3).reshape(Y, 16, cols)
    return lax.dynamic_slice_in_dim(jnp.concatenate([part, part]), y, Y, 0)


def half_kernel(core, *refs):
    pieces, weight_ref = refs[:Y], refs[Y]
    rows = [p[core * X : core * X + X].reshape(X * 16, p.shape[-1]) for p in pieces]
    part = jnp.dot(jnp.concatenate(rows), weight_ref[...], preferred_element_type=F32)
    if core == 1:
        refs[Y + 1][...] = part
        return
    theirs_ref, own_ref, sent_refs = refs[Y + 1], refs[Y + 2], refs[Y + 3 :]
    part = (part + theirs_ref[...]).reshape(Y, X, 16, part.shape[-1])
    own_ref[...] = part[:, 0]
    for j in range(1, X):
        sent_refs[j - 1][...] = part[:, j].astype(BF)


def half_dot(core, pieces, weight, theirs=()):
    width, cols = weight.shape
    shape = jax.ShapeDtypeStruct((256, cols), F32)
    if core == 0:
        block = (Y, 16, cols)
        shape = [jax.ShapeDtypeStruct(block, F32)] + [jax.ShapeDtypeStruct(block, BF)] * (X - 1)
    vmem = pl.BlockSpec(memory_space=pltpu.VMEM)
    return pl.pallas_call(
        functools.partial(half_kernel, core),
        out_shape=shape,
        in_specs=[vmem] * (Y + 1 + len(theirs)),
        out_specs=jax.tree.map(lambda _: vmem, shape),
        compiler_params=pltpu.CompilerParams(vmem_limit_bytes=8 * MIB),
        cost_estimate=pl.CostEstimate(
            flops=2 * 256 * width * cols, bytes_accessed=2 * width * cols, transcendentals=0
        ),
        name=f"half_{core}",
    )(*pieces, weight, *theirs)


def gate_kernel(mine_ref, other_ref, factor_ref, hidden_ref):
    cols = hidden_ref.shape[-1]
    start = lax.axis_index("tensor") * cols
    granule = lax.broadcasted_iota(jnp.int32, (16, cols), 0) // 4
    live = start < lax.shift_right_logical(FF, G - 1 - granule)

    def step(i, carry):
        x, j = i // Y, lax.rem(i, Y)
        for c, ref in enumerate((mine_ref, other_ref)):
            gate, up = ref[x, 0, j].astype(F32), ref[x, 1, j].astype(F32)
            sig = 1.0 / (1.0 + jnp.exp(-gate))
            active = jnp.where(live, gate * sig, 0.0)
            rows = pl.ds(pl.multiple_of((j * Z + c * X + x) * 16, 16), 16)
            factor_ref[0, rows, :] = jnp.where(live, up * sig * (1.0 + gate * (1.0 - sig)), 0.0)
            factor_ref[1, rows, :] = active
            hidden_ref[rows, :] = (active * up).astype(BF)
        return carry

    lax.fori_loop(0, X * Y, step, 0)


def gate_terms(mine, other):
    cols = mine.shape[-1]
    vmem = pl.BlockSpec(memory_space=pltpu.VMEM)
    return pl.pallas_call(
        gate_kernel,
        out_shape=[jax.ShapeDtypeStruct((2, 512, cols), F32), jax.ShapeDtypeStruct((512, cols), BF)],
        in_specs=[vmem] * 2,
        out_specs=[vmem] * 2,
        compiler_params=pltpu.CompilerParams(vmem_limit_bytes=4 * MIB),
        cost_estimate=pl.CostEstimate(
            flops=16 * 512 * cols, bytes_accessed=12 * 512 * cols, transcendentals=512 * cols
        ),
        name="gate_terms",
    )(mine, other)


def input_kernel(*refs):
    pieces, (factor_ref, gate_ref, up_ref), (rows_ref, own_ref), sent_refs = (
        refs[:Z],
        refs[Z : Z + 3],
        refs[Z + 3 : Z + 5],
        refs[Z + 5 :],
    )
    for k in range(Z):
        for j in range(Y):
            rows = pl.ds((j * Z + k) * 16, 16)
            dhid = pieces[k][j].astype(F32)
            for array in range(2):
                rows_ref[array, rows, :] = (dhid * factor_ref[array, rows, :]).astype(BF)
    for start in range(0, own_ref.shape[1], 256):
        lanes = pl.ds(start, 256)
        term = cols_dot(rows_ref[0], gate_ref[lanes, :]) + cols_dot(rows_ref[1], up_ref[lanes, :])
        own_ref[:, lanes] = term[:128]
        for j in range(1, Y):
            sent_refs[j - 1][:, lanes] = term[128 * j : 128 * j + 128].astype(BF)


def input_terms(pieces, factors, gate_weight, up_weight):
    width, cols = gate_weight.shape
    vmem = pl.BlockSpec(memory_space=pltpu.VMEM)
    return pl.pallas_call(
        input_kernel,
        out_shape=[
            jax.ShapeDtypeStruct((2, 512, cols), BF),
            jax.ShapeDtypeStruct((128, width), F32),
        ]
        + [jax.ShapeDtypeStruct((128, width), BF)] * (Y - 1),
        in_specs=[vmem] * (Z + 3),
        out_specs=[vmem] * (Y + 1),
        compiler_params=pltpu.CompilerParams(vmem_limit_bytes=10 * MIB),
        cost_estimate=pl.CostEstimate(
            flops=4 * 512 * width * cols, bytes_accessed=4 * width * cols, transcendentals=0
        ),
        name="input_terms",
    )(*pieces, factors, gate_weight, up_weight)


def weight_kernel(*refs):
    in_refs, grad_refs, (hidden_ref, rows_ref) = refs[:Y], refs[Y : 2 * Y], refs[2 * Y : 2 * Y + 2]
    outs, (blocks, sems) = refs[2 * Y + 2 : 2 * Y + 5], refs[2 * Y + 5 :]
    def copy(k, i):
        band = pl.ds(pl.multiple_of(i * BAND, BAND), BAND)
        return pltpu.make_async_copy(blocks.at[k, band], outs[k].at[band], sems.at[k, i])

    def step(i, carry):
        band = pl.ds(pl.multiple_of(i * BAND, BAND), BAND)
        ins, grads = (
            jnp.concatenate([r[:, :, band].reshape(Z * 16, BAND) for r in pieces])
            for pieces in (in_refs, grad_refs)
        )
        for k, (left, right) in enumerate(((ins, rows_ref[0]), (ins, rows_ref[1]), (grads, hidden_ref[...]))):
            blocks[k, band, :] = rows_dot(left, right).astype(BF)
            copy(k, i).start()
        return carry

    bands = in_refs[0].shape[-1] // BAND
    lax.fori_loop(0, bands, step, 0)
    for i in range(bands):
        for k in range(3):
            copy(k, i).wait()


def weight_grads(in_y, grad_y, hidden, rows):
    width, cols = in_y[0].shape[-1], rows.shape[-1]
    vmem = pl.BlockSpec(memory_space=pltpu.VMEM)
    return pl.pallas_call(
        weight_kernel,
        out_shape=[jax.ShapeDtypeStruct((width, cols), BF)] * 3,
        in_specs=[vmem] * (2 * Y + 2),
        out_specs=[pl.BlockSpec(memory_space=pl.ANY)] * 3,
        scratch_shapes=[
            pltpu.VMEM((3, width, cols), BF),
            pltpu.SemaphoreType.DMA((3, width // BAND)),
        ],
        compiler_params=pltpu.CompilerParams(vmem_limit_bytes=14 * MIB),
        cost_estimate=pl.CostEstimate(
            flops=6 * 512 * width * cols, bytes_accessed=6 * width * cols, transcendentals=0
        ),
        name="weight_grads",
    )(*in_y, *grad_y, hidden, rows)


def shards(inputs, grad_out, gate_pre, up_pre, gate_weight, up_weight, down_weight):
    width, cols = gate_weight.shape
    tensor = lax.axis_index("tensor")
    both = exchange_z(jnp.broadcast_to(jnp.stack([grad_out, inputs]), (Z, 2, G, 4, width)))
    both = both.reshape(Z, 2, 16, width)

    pre = jnp.stack([own_tokens(gate_pre, tensor % Y), own_tokens(up_pre, tensor % Y)])
    pre = [pre] + [from_x(pre, j) for j in range(1, X)]
    both, pre = lax.optimization_barrier((both, pre))
    grad_z, in_z = both[:, 0], both[:, 1]
    grad_y = [grad_z] + [from_y(grad_z, j) for j in range(1, Y)]

    pre = jnp.stack(pre)
    factors, hidden = gate_terms(pre, swap_core(pre))
    theirs, in_z = lax.optimization_barrier((half_dot(1, grad_y, down_weight), in_z))
    theirs = swap_core(theirs)
    dhid, *blocks = half_dot(0, grad_y, down_weight, (theirs,))
    blocks = [from_x(blocks[j - 1], -j) for j in range(1, X)]
    in_y = [in_z] + [from_y(in_z, j) for j in range(1, Y)]
    blocks, factors, hidden, in_y[1] = lax.optimization_barrier((blocks, factors, hidden, in_y[1]))
    for block in blocks:
        dhid = dhid + block.astype(F32)

    d_own = dhid.astype(BF)
    d_x = [d_own] + [from_x(d_own, j) for j in range(1, X)]
    d_other = [swap_core(d) for d in d_x]
    d_other, in_y = lax.optimization_barrier((d_other, in_y))

    rows, own, *sent = input_terms(d_x + d_other, factors, gate_weight, up_weight)
    sent, hidden = lax.optimization_barrier((sent, hidden))
    total = own
    for j in range(1, Y):
        total = total + from_y(sent[j - 1], -j).astype(F32)
    total, rows, grad_y, in_y, hidden = lax.optimization_barrier(
        (total.astype(BF), rows, grad_y, in_y, hidden)
    )
    total = exchange_z(total.reshape(Z, 16, width))
    gate_grad, up_grad, down_grad = weight_grads(in_y, grad_y, hidden, rows)
    in_grads = total.astype(F32).sum(0).astype(BF).reshape(G, 4, width)
    return in_grads, gate_grad, up_grad, down_grad


def solution(mesh):
    tokens = P(None, "tensor", "dp")
    hidden = P(None, "dp", "tensor")
    weight = P("dp", "tensor")
    return jax.shard_map(
        shards,
        mesh=mesh,
        in_specs=(tokens, tokens, hidden, hidden, weight, weight, weight),
        out_specs=(tokens, weight, weight, weight),
        check_vma=False,
    )
```

```python
import functools

import jax
import jax.numpy as jnp
from jax import lax
from jax.experimental import pallas as pl
from jax.experimental.pallas import tpu as pltpu
from jax.sharding import PartitionSpec as P

FF = 28672
G = 4
X, C, Y, Z = 4, 2, 4, 8
BF = jnp.bfloat16
F32 = jnp.float32
MIB = 1024 * 1024
BAND = 256
Z_GROUPS = [
    [(x * C + c) * Y * Z + ((x + dx) % X * C + (c ^ dc)) * Y + y for dc in range(C) for dx in range(X)]
    for x in range(X)
    for c in range(C)
    for y in range(Y)
]
CORE_SWAP = [(d, d ^ 1) for d in range(X * C)]


def from_x(block, step):
    return lax.ppermute(block, "dp", [((d // C + step) % X * C + d % C, d) for d in range(X * C)])


def from_y(block, step):
    return lax.ppermute(block, "tensor", [(t // Y * Y + (t % Y + step) % Y, t) for t in range(Y * Z)])


def swap_core(block):
    return lax.ppermute(block, "dp", CORE_SWAP)


def exchange_z(blocks):
    return lax.all_to_all(blocks, ("dp", "tensor"), 0, 0, axis_index_groups=Z_GROUPS)


def rows_dot(left, right):
    return lax.dot_general(left, right, (((0,), (0,)), ((), ())), preferred_element_type=F32)


def cols_dot(left, right):
    return lax.dot_general(left, right, (((1,), (1,)), ((), ())), preferred_element_type=F32)


def own_tokens(part, y):
    cols = part.shape[-1]
    part = part.reshape(G, Y, 4, cols).transpose(1, 0, 2, 3).reshape(Y, 16, cols)
    return lax.dynamic_slice_in_dim(jnp.concatenate([part, part]), y, Y, 0)


def half_kernel(core, *refs):
    pieces, weight_ref = refs[:Y], refs[Y]
    rows = [p[core * X : core * X + X].reshape(X * 16, p.shape[-1]) for p in pieces]
    part = jnp.dot(jnp.concatenate(rows), weight_ref[...], preferred_element_type=F32)
    if core == 1:
        refs[Y + 1][...] = part
        return
    theirs_ref, own_ref, sent_refs = refs[Y + 1], refs[Y + 2], refs[Y + 3 :]
    part = (part + theirs_ref[...]).reshape(Y, X, 16, part.shape[-1])
    own_ref[...] = part[:, 0]
    for j in range(1, X):
        sent_refs[j - 1][...] = part[:, j].astype(BF)


def half_dot(core, pieces, weight, theirs=()):
    width, cols = weight.shape
    shape = jax.ShapeDtypeStruct((256, cols), F32)
    if core == 0:
        block = (Y, 16, cols)
        shape = [jax.ShapeDtypeStruct(block, F32)] + [jax.ShapeDtypeStruct(block, BF)] * (X - 1)
    vmem = pl.BlockSpec(memory_space=pltpu.VMEM)
    return pl.pallas_call(
        functools.partial(half_kernel, core),
        out_shape=shape,
        in_specs=[vmem] * (Y + 1 + len(theirs)),
        out_specs=jax.tree.map(lambda _: vmem, shape),
        compiler_params=pltpu.CompilerParams(vmem_limit_bytes=8 * MIB),
        cost_estimate=pl.CostEstimate(
            flops=2 * 256 * width * cols, bytes_accessed=2 * width * cols, transcendentals=0
        ),
        name=f"half_{core}",
    )(*pieces, weight, *theirs)


def gate_kernel(mine_ref, other_ref, factor_ref, hidden_ref):
    cols = hidden_ref.shape[-1]
    start = lax.axis_index("tensor") * cols
    granule = lax.broadcasted_iota(jnp.int32, (16, cols), 0) // 4
    live = start < lax.shift_right_logical(FF, G - 1 - granule)

    def step(i, carry):
        x, j = i // Y, lax.rem(i, Y)
        for c, ref in enumerate((mine_ref, other_ref)):
            gate, up = ref[x, 0, j].astype(F32), ref[x, 1, j].astype(F32)
            sig = 1.0 / (1.0 + jnp.exp(-gate))
            active = jnp.where(live, gate * sig, 0.0)
            rows = pl.ds(pl.multiple_of((j * Z + c * X + x) * 16, 16), 16)
            factor_ref[0, rows, :] = jnp.where(live, up * sig * (1.0 + gate * (1.0 - sig)), 0.0)
            factor_ref[1, rows, :] = active
            hidden_ref[rows, :] = (active * up).astype(BF)
        return carry

    lax.fori_loop(0, X * Y, step, 0)


def gate_terms(mine, other):
    cols = mine.shape[-1]
    vmem = pl.BlockSpec(memory_space=pltpu.VMEM)
    return pl.pallas_call(
        gate_kernel,
        out_shape=[jax.ShapeDtypeStruct((2, 512, cols), F32), jax.ShapeDtypeStruct((512, cols), BF)],
        in_specs=[vmem] * 2,
        out_specs=[vmem] * 2,
        compiler_params=pltpu.CompilerParams(vmem_limit_bytes=4 * MIB),
        cost_estimate=pl.CostEstimate(
            flops=16 * 512 * cols, bytes_accessed=12 * 512 * cols, transcendentals=512 * cols
        ),
        name="gate_terms",
    )(mine, other)


def input_kernel(*refs):
    pieces, (factor_ref, gate_ref, up_ref), (rows_ref, own_ref), sent_refs = (
        refs[:Z],
        refs[Z : Z + 3],
        refs[Z + 3 : Z + 5],
        refs[Z + 5 :],
    )
    for k in range(Z):
        for j in range(Y):
            rows = pl.ds((j * Z + k) * 16, 16)
            dhid = pieces[k][j].astype(F32)
            for array in range(2):
                rows_ref[array, rows, :] = (dhid * factor_ref[array, rows, :]).astype(BF)
    for start in range(0, own_ref.shape[1], 256):
        lanes = pl.ds(start, 256)
        term = cols_dot(rows_ref[0], gate_ref[lanes, :]) + cols_dot(rows_ref[1], up_ref[lanes, :])
        own_ref[:, lanes] = term[:128]
        for j in range(1, Y):
            sent_refs[j - 1][:, lanes] = term[128 * j : 128 * j + 128].astype(BF)


def input_terms(pieces, factors, gate_weight, up_weight):
    width, cols = gate_weight.shape
    vmem = pl.BlockSpec(memory_space=pltpu.VMEM)
    return pl.pallas_call(
        input_kernel,
        out_shape=[
            jax.ShapeDtypeStruct((2, 512, cols), BF),
            jax.ShapeDtypeStruct((128, width), F32),
        ]
        + [jax.ShapeDtypeStruct((128, width), BF)] * (Y - 1),
        in_specs=[vmem] * (Z + 3),
        out_specs=[vmem] * (Y + 1),
        compiler_params=pltpu.CompilerParams(vmem_limit_bytes=10 * MIB),
        cost_estimate=pl.CostEstimate(
            flops=4 * 512 * width * cols, bytes_accessed=4 * width * cols, transcendentals=0
        ),
        name="input_terms",
    )(*pieces, factors, gate_weight, up_weight)


def weight_kernel(*refs):
    in_refs, grad_refs, (hidden_ref, rows_ref) = refs[:Y], refs[Y : 2 * Y], refs[2 * Y : 2 * Y + 2]
    outs, (blocks, sems) = refs[2 * Y + 2 : 2 * Y + 5], refs[2 * Y + 5 :]
    def copy(k, i):
        band = pl.ds(pl.multiple_of(i * BAND, BAND), BAND)
        return pltpu.make_async_copy(blocks.at[k, band], outs[k].at[band], sems.at[k, i])

    def step(i, carry):
        band = pl.ds(pl.multiple_of(i * BAND, BAND), BAND)
        ins, grads = (
            jnp.concatenate([r[:, :, band].reshape(Z * 16, BAND) for r in pieces])
            for pieces in (in_refs, grad_refs)
        )
        for k, (left, right) in enumerate(((ins, rows_ref[0]), (ins, rows_ref[1]), (grads, hidden_ref[...]))):
            blocks[k, band, :] = rows_dot(left, right).astype(BF)
            copy(k, i).start()
        return carry

    bands = in_refs[0].shape[-1] // BAND
    lax.fori_loop(0, bands, step, 0)
    for i in range(bands):
        for k in range(3):
            copy(k, i).wait()


def weight_grads(in_y, grad_y, hidden, rows):
    width, cols = in_y[0].shape[-1], rows.shape[-1]
    vmem = pl.BlockSpec(memory_space=pltpu.VMEM)
    return pl.pallas_call(
        weight_kernel,
        out_shape=[jax.ShapeDtypeStruct((width, cols), BF)] * 3,
        in_specs=[vmem] * (2 * Y + 2),
        out_specs=[pl.BlockSpec(memory_space=pl.ANY)] * 3,
        scratch_shapes=[
            pltpu.VMEM((3, width, cols), BF),
            pltpu.SemaphoreType.DMA((3, width // BAND)),
        ],
        compiler_params=pltpu.CompilerParams(vmem_limit_bytes=14 * MIB),
        cost_estimate=pl.CostEstimate(
            flops=6 * 512 * width * cols, bytes_accessed=6 * width * cols, transcendentals=0
        ),
        name="weight_grads",
    )(*in_y, *grad_y, hidden, rows)


def shards(inputs, grad_out, gate_pre, up_pre, gate_weight, up_weight, down_weight):
    width, cols = gate_weight.shape
    tensor = lax.axis_index("tensor")
    both = exchange_z(jnp.broadcast_to(jnp.stack([grad_out, inputs]), (Z, 2, G, 4, width)))
    both = both.reshape(Z, 2, 16, width)

    pre = jnp.stack([own_tokens(gate_pre, tensor % Y), own_tokens(up_pre, tensor % Y)])
    pre = [pre] + [from_x(pre, j) for j in range(1, X)]
    both, pre = lax.optimization_barrier((both, jnp.stack(pre)))
    grad_z, in_z = both[:, 0], both[:, 1]
    grad_y = [grad_z] + [from_y(grad_z, j) for j in range(1, Y)]

    factors, hidden = gate_terms(pre, swap_core(pre))
    grad_y, factors, hidden = lax.optimization_barrier((grad_y, factors, hidden))
    theirs, in_z = lax.optimization_barrier((half_dot(1, grad_y, down_weight), in_z))
    theirs = swap_core(theirs)
    dhid, *blocks = half_dot(0, grad_y, down_weight, (theirs,))
    blocks = [from_x(blocks[j - 1], -j) for j in range(1, X)]
    in_y = [in_z] + [from_y(in_z, j) for j in range(1, Y)]
    blocks, in_y[1] = lax.optimization_barrier((blocks, in_y[1]))
    for block in blocks:
        dhid = dhid + block.astype(F32)

    d_own = dhid.astype(BF)
    d_x = [d_own] + [from_x(d_own, j) for j in range(1, X)]
    d_other = [swap_core(d) for d in d_x]
    d_other, in_y = lax.optimization_barrier((d_other, in_y))

    rows, own, *sent = input_terms(d_x + d_other, factors, gate_weight, up_weight)
    sent, hidden = lax.optimization_barrier((sent, hidden))
    total = own
    for j in range(1, Y):
        total = total + from_y(sent[j - 1], -j).astype(F32)
    total, rows, grad_y, in_y, hidden = lax.optimization_barrier(
        (total.astype(BF), rows, grad_y, in_y, hidden)
    )
    total = exchange_z(total.reshape(Z, 16, width))
    gate_grad, up_grad, down_grad = weight_grads(in_y, grad_y, hidden, rows)
    in_grads = total.astype(F32).sum(0).astype(BF).reshape(G, 4, width)
    return in_grads, gate_grad, up_grad, down_grad


def solution(mesh):
    tokens = P(None, "tensor", "dp")
    hidden = P(None, "dp", "tensor")
    weight = P("dp", "tensor")
    return jax.shard_map(
        shards,
        mesh=mesh,
        in_specs=(tokens, tokens, hidden, hidden, weight, weight, weight),
        out_specs=(tokens, weight, weight, weight),
        check_vma=False,
    )
```

```python
import functools

import jax
import jax.numpy as jnp
from jax import lax
from jax.experimental import pallas as pl
from jax.experimental.pallas import tpu as pltpu
from jax.sharding import PartitionSpec as P

FF = 28672
G = 4
X, C, Y, Z = 4, 2, 4, 8
BF = jnp.bfloat16
F32 = jnp.float32
MIB = 1024 * 1024
BAND = 256
Z_GROUPS = [
    [(x * C + c) * Y * Z + ((x + dx) % X * C + (c ^ dc)) * Y + y for dc in range(C) for dx in range(X)]
    for x in range(X)
    for c in range(C)
    for y in range(Y)
]
CORE_SWAP = [(d, d ^ 1) for d in range(X * C)]


def from_x(block, step):
    return lax.ppermute(block, "dp", [((d // C + step) % X * C + d % C, d) for d in range(X * C)])


def from_y(block, step):
    return lax.ppermute(block, "tensor", [(t // Y * Y + (t % Y + step) % Y, t) for t in range(Y * Z)])


def swap_core(block):
    return lax.ppermute(block, "dp", CORE_SWAP)


def exchange_z(blocks):
    return lax.all_to_all(blocks, ("dp", "tensor"), 0, 0, axis_index_groups=Z_GROUPS)


def rows_dot(left, right):
    return lax.dot_general(left, right, (((0,), (0,)), ((), ())), preferred_element_type=F32)


def cols_dot(left, right):
    return lax.dot_general(left, right, (((1,), (1,)), ((), ())), preferred_element_type=F32)


def own_tokens(part, y):
    cols = part.shape[-1]
    part = part.reshape(G, Y, 4, cols).transpose(1, 0, 2, 3).reshape(Y, 16, cols)
    return lax.dynamic_slice_in_dim(jnp.concatenate([part, part]), y, Y, 0)


def half_kernel(core, *refs):
    pieces, weight_ref = refs[:Y], refs[Y]
    rows = [p[core * X : core * X + X].reshape(X * 16, p.shape[-1]) for p in pieces]
    part = jnp.dot(jnp.concatenate(rows), weight_ref[...], preferred_element_type=F32)
    if core == 1:
        refs[Y + 1][...] = part
        return
    theirs_ref, own_ref, sent_refs = refs[Y + 1], refs[Y + 2], refs[Y + 3 :]
    part = (part + theirs_ref[...]).reshape(Y, X, 16, part.shape[-1])
    own_ref[...] = part[:, 0]
    for j in range(1, X):
        sent_refs[j - 1][...] = part[:, j].astype(BF)


def half_dot(core, pieces, weight, theirs=()):
    width, cols = weight.shape
    shape = jax.ShapeDtypeStruct((256, cols), F32)
    if core == 0:
        block = (Y, 16, cols)
        shape = [jax.ShapeDtypeStruct(block, F32)] + [jax.ShapeDtypeStruct(block, BF)] * (X - 1)
    vmem = pl.BlockSpec(memory_space=pltpu.VMEM)
    return pl.pallas_call(
        functools.partial(half_kernel, core),
        out_shape=shape,
        in_specs=[vmem] * (Y + 1 + len(theirs)),
        out_specs=jax.tree.map(lambda _: vmem, shape),
        compiler_params=pltpu.CompilerParams(vmem_limit_bytes=8 * MIB),
        cost_estimate=pl.CostEstimate(
            flops=2 * 256 * width * cols, bytes_accessed=2 * width * cols, transcendentals=0
        ),
        name=f"half_{core}",
    )(*pieces, weight, *theirs)


def gate_kernel(mine_ref, other_ref, factor_ref, hidden_ref):
    cols = hidden_ref.shape[-1]
    start = lax.axis_index("tensor") * cols
    granule = lax.broadcasted_iota(jnp.int32, (16, cols), 0) // 4
    live = start < lax.shift_right_logical(FF, G - 1 - granule)

    def step(i, carry):
        x, j = i // Y, lax.rem(i, Y)
        for c, ref in enumerate((mine_ref, other_ref)):
            gate, up = ref[x, 0, j].astype(F32), ref[x, 1, j].astype(F32)
            sig = 1.0 / (1.0 + jnp.exp(-gate))
            active = jnp.where(live, gate * sig, 0.0)
            rows = pl.ds(pl.multiple_of((j * Z + c * X + x) * 16, 16), 16)
            factor_ref[0, rows, :] = jnp.where(live, up * sig * (1.0 + gate * (1.0 - sig)), 0.0)
            factor_ref[1, rows, :] = active
            hidden_ref[rows, :] = (active * up).astype(BF)
        return carry

    lax.fori_loop(0, X * Y, step, 0)


def gate_terms(mine, other):
    cols = mine.shape[-1]
    vmem = pl.BlockSpec(memory_space=pltpu.VMEM)
    return pl.pallas_call(
        gate_kernel,
        out_shape=[jax.ShapeDtypeStruct((2, 512, cols), F32), jax.ShapeDtypeStruct((512, cols), BF)],
        in_specs=[vmem] * 2,
        out_specs=[vmem] * 2,
        compiler_params=pltpu.CompilerParams(vmem_limit_bytes=4 * MIB),
        cost_estimate=pl.CostEstimate(
            flops=16 * 512 * cols, bytes_accessed=12 * 512 * cols, transcendentals=512 * cols
        ),
        name="gate_terms",
    )(mine, other)


def input_kernel(*refs):
    pieces, (factor_ref, gate_ref, up_ref), (rows_ref, own_ref), sent_refs = (
        refs[:Z],
        refs[Z : Z + 3],
        refs[Z + 3 : Z + 5],
        refs[Z + 5 :],
    )
    for k in range(Z):
        for j in range(Y):
            rows = pl.ds((j * Z + k) * 16, 16)
            dhid = pieces[k][j].astype(F32)
            for array in range(2):
                rows_ref[array, rows, :] = (dhid * factor_ref[array, rows, :]).astype(BF)
    for start in range(0, own_ref.shape[1], 256):
        lanes = pl.ds(start, 256)
        term = cols_dot(rows_ref[0], gate_ref[lanes, :]) + cols_dot(rows_ref[1], up_ref[lanes, :])
        own_ref[:, lanes] = term[:128]
        for j in range(1, Y):
            sent_refs[j - 1][:, lanes] = term[128 * j : 128 * j + 128].astype(BF)


def input_terms(pieces, factors, gate_weight, up_weight):
    width, cols = gate_weight.shape
    vmem = pl.BlockSpec(memory_space=pltpu.VMEM)
    return pl.pallas_call(
        input_kernel,
        out_shape=[
            jax.ShapeDtypeStruct((2, 512, cols), BF),
            jax.ShapeDtypeStruct((128, width), F32),
        ]
        + [jax.ShapeDtypeStruct((128, width), BF)] * (Y - 1),
        in_specs=[vmem] * (Z + 3),
        out_specs=[vmem] * (Y + 1),
        compiler_params=pltpu.CompilerParams(vmem_limit_bytes=10 * MIB),
        cost_estimate=pl.CostEstimate(
            flops=4 * 512 * width * cols, bytes_accessed=4 * width * cols, transcendentals=0
        ),
        name="input_terms",
    )(*pieces, factors, gate_weight, up_weight)


def weight_kernel(*refs):
    in_refs, grad_refs, (hidden_ref, rows_ref) = refs[:Y], refs[Y : 2 * Y], refs[2 * Y : 2 * Y + 2]
    outs, (blocks, sems) = refs[2 * Y + 2 : 2 * Y + 5], refs[2 * Y + 5 :]
    def copy(k, i):
        band = pl.ds(pl.multiple_of(i * BAND, BAND), BAND)
        return pltpu.make_async_copy(blocks.at[k, band], outs[k].at[band], sems.at[k, i])

    def step(i, carry):
        band = pl.ds(pl.multiple_of(i * BAND, BAND), BAND)
        ins, grads = (
            jnp.concatenate([r[:, :, band].reshape(Z * 16, BAND) for r in pieces])
            for pieces in (in_refs, grad_refs)
        )
        for k, (left, right) in enumerate(((ins, rows_ref[0]), (ins, rows_ref[1]), (grads, hidden_ref[...]))):
            blocks[k, band, :] = rows_dot(left, right).astype(BF)
            copy(k, i).start()
        return carry

    bands = in_refs[0].shape[-1] // BAND
    lax.fori_loop(0, bands, step, 0)
    for i in range(bands):
        for k in range(3):
            copy(k, i).wait()


def weight_grads(in_y, grad_y, hidden, rows):
    width, cols = in_y[0].shape[-1], rows.shape[-1]
    vmem = pl.BlockSpec(memory_space=pltpu.VMEM)
    return pl.pallas_call(
        weight_kernel,
        out_shape=[jax.ShapeDtypeStruct((width, cols), BF)] * 3,
        in_specs=[vmem] * (2 * Y + 2),
        out_specs=[pl.BlockSpec(memory_space=pl.ANY)] * 3,
        scratch_shapes=[
            pltpu.VMEM((3, width, cols), BF),
            pltpu.SemaphoreType.DMA((3, width // BAND)),
        ],
        compiler_params=pltpu.CompilerParams(vmem_limit_bytes=14 * MIB),
        cost_estimate=pl.CostEstimate(
            flops=6 * 512 * width * cols, bytes_accessed=6 * width * cols, transcendentals=0
        ),
        name="weight_grads",
    )(*in_y, *grad_y, hidden, rows)


def shards(inputs, grad_out, gate_pre, up_pre, gate_weight, up_weight, down_weight):
    width, cols = gate_weight.shape
    tensor = lax.axis_index("tensor")
    both = exchange_z(jnp.broadcast_to(jnp.stack([grad_out, inputs]), (Z, 2, G, 4, width)))
    both = both.reshape(Z, 2, 16, width)

    pre = jnp.stack([own_tokens(gate_pre, tensor % Y), own_tokens(up_pre, tensor % Y)])
    pre = [pre] + [from_x(pre, j) for j in range(1, X)]
    both, pre = lax.optimization_barrier((both, jnp.stack(pre)))
    grad_z, in_z = both[:, 0], both[:, 1]
    grad_y = [grad_z] + [from_y(grad_z, j) for j in range(1, Y)]

    factors, hidden = gate_terms(pre, swap_core(pre))
    grad_y, factors, hidden = lax.optimization_barrier((grad_y, factors, hidden))
    theirs, in_z = lax.optimization_barrier((half_dot(1, grad_y, down_weight), in_z))
    theirs = swap_core(theirs)
    dhid, *blocks = half_dot(0, grad_y, down_weight, (theirs,))
    blocks = [from_x(blocks[j - 1], -j) for j in range(1, X)]
    in_y = [in_z] + [from_y(in_z, j) for j in range(1, Y)]
    for block in blocks:
        dhid = dhid + block.astype(F32)

    d_own = dhid.astype(BF)
    d_x = [d_own] + [from_x(d_own, j) for j in range(1, X)]
    d_x[1], in_y = lax.optimization_barrier((d_x[1], in_y))
    d_other = [swap_core(d) for d in d_x]

    rows, own, *sent = input_terms(d_x + d_other, factors, gate_weight, up_weight)
    sent, hidden = lax.optimization_barrier((sent, hidden))
    total = own
    for j in range(1, Y):
        total = total + from_y(sent[j - 1], -j).astype(F32)
    total, rows, grad_y, in_y, hidden = lax.optimization_barrier(
        (total.astype(BF), rows, grad_y, in_y, hidden)
    )
    total = exchange_z(total.reshape(Z, 16, width))
    gate_grad, up_grad, down_grad = weight_grads(in_y, grad_y, hidden, rows)
    in_grads = total.astype(F32).sum(0).astype(BF).reshape(G, 4, width)
    return in_grads, gate_grad, up_grad, down_grad


def solution(mesh):
    tokens = P(None, "tensor", "dp")
    hidden = P(None, "dp", "tensor")
    weight = P("dp", "tensor")
    return jax.shard_map(
        shards,
        mesh=mesh,
        in_specs=(tokens, tokens, hidden, hidden, weight, weight, weight),
        out_specs=(tokens, weight, weight, weight),
        check_vma=False,
    )
```
